256 devices in a mesh: ctx: 16 (over z, core), head: 4 (over x), dp: 4 (over y).
Axes of the slice: x: 4, y: 4, z: 8, core: 2. Of those that a mesh axis runs over, the one named last changes fastest.
Arguments:
- queries: bfloat16 [32768, 4096], P(('dp', 'ctx'), 'head'), parts along dimension 0, may hold values from -6 to 6
- keys: bfloat16 [32768, 4096], P(('dp', 'ctx'), 'head'), parts along dimension 0, may hold values from -6 to 6
- values: bfloat16 [32768, 4096], P(('dp', 'ctx'), 'head'), parts along dimension 0, may hold values from -6 to 6
- out_grad: bfloat16 [32768, 4096], P(('dp', 'ctx'), 'head'), parts along dimension 0, may hold values from -1.1953125 to 1.1953125
- forward_out: bfloat16 [32768, 4096], P(('dp', 'ctx'), 'head'), parts along dimension 0, may hold values from -6 to 6
- log_norm: float32 [32, 32768], P('head', ('dp', 'ctx')), parts along dimension 1, may hold values from 6 to 8
- beacon_keys: bfloat16 [4096, 4096], P(('dp', 'ctx'), 'head'), parts along dimension 0, may hold values from -6 to 6
- beacon_values: bfloat16 [4096, 4096], P(('dp', 'ctx'), 'head'), parts along dimension 0, may hold values from -6 to 6
- beacon_reach: int32 [64], P(('dp', 'ctx')), parts along dimension 0, may hold values from 1 to 16
Outputs:
- query_grad: bfloat16 [32768, 4096], P(('dp', 'ctx'), 'head'), parts along dimension 0
- key_grad: bfloat16 [32768, 4096], P(('dp', 'ctx'), 'head'), parts along dimension 0
- value_grad: bfloat16 [32768, 4096], P(('dp', 'ctx'), 'head'), parts along dimension 0
- beacon_key_grad: bfloat16 [4096, 4096], P(('dp', 'ctx'), 'head'), parts along dimension 0
- beacon_value_grad: bfloat16 [4096, 4096], P(('dp', 'ctx'), 'head'), parts along dimension 0
The draws below stay inside these ranges and needn't reach their ends.
There are 4 independent parts, one for each index of `dp`. The reference program is written for one: setup_inputs(seed, part) draws one part's arguments, and reference() takes and returns one part's arrays. A program takes and returns all parts, laid end to end along the dimension named above; each array names one. Nothing has to cross between parts.
All inputs are finite; a program needn't handle non-finite values.
Results may differ from the reference program's by a relative error of at most 0.0054.
Values may be sent and summed in bfloat16 or wider, within the bound.
No kernel may reach another device: no remote copies, remote signals or barrier semaphores. Data moves between devices by JAX's collectives and lax.ppermute only.
A program may use at most 128 MiB of HBM per device.

```python
import math
import jax
import jax.numpy as jnp
from jax import lax

HD = 128
HEADS = 32
GROUP = 512
BPC = 64
TOKENS = 8192
BEACONS = 1024
GROUPS = 16


def with_ends(entries, key, low, largest):
    longest = entries.shape.index(max(entries.shape))
    spots = []
    for shift in (0, 1):
        where = [jax.random.randint(jax.random.fold_in(key, axis), (), 0, length) for axis, length in enumerate(entries.shape)]
        where[longest] = (where[longest] + shift) % entries.shape[longest]
        spots.append(tuple(where))
    return entries.at[spots[0]].set(low).at[spots[1]].set(largest)


def block_scale(key, shape, pieces, least, largest):
    def one(axis_at, blocks):
        draws = jax.random.uniform(jax.random.fold_in(jax.random.fold_in(key, 6), axis_at), (blocks,), jnp.float32, least / len(pieces), largest / len(pieces))
        return jnp.repeat(jnp.exp(draws), shape[axis_at] // blocks).reshape((-1,) + (1,) * (len(shape) - axis_at - 1))

    loudness = one(*pieces[0])
    for cut in pieces[1:]:
        loudness = loudness * one(*cut)
    return loudness


def gaussian(own_key, shape, width, bound, split=(), kind=jnp.bfloat16):
    values = width * jax.random.normal(own_key, shape, jnp.float32)
    if split:
        values = values * block_scale(own_key, shape, split, -0.22, 0.18)
    return jnp.clip(values, -bound, bound).astype(kind)


def setup_inputs(seed: int = 0, part: int = 0) -> dict:
    streams_of = jax.random.split(jax.random.key(seed), 10)
    part_keys = jax.random.split(jax.random.fold_in(streams_of[9], part), 10)
    queries = gaussian(part_keys[0], (TOKENS, HEADS * HD), 1.0, 6.0, ((0, 16), (1, 4)))
    keys = gaussian(part_keys[1], (TOKENS, HEADS * HD), 1.0, 6.0, ((0, 16), (1, 4)))
    values = gaussian(part_keys[2], (TOKENS, HEADS * HD), 1.0, 6.0, ((0, 16), (1, 4)))
    out_grad = gaussian(part_keys[3], (TOKENS, HEADS * HD), 0.2, 1.1953125, ((0, 16), (1, 4)))
    forward_out = gaussian(part_keys[4], (TOKENS, HEADS * HD), 1.0, 6.0, ((0, 16), (1, 4)))
    log_norm = jnp.clip(6.0 + 2.0 * jax.random.uniform(part_keys[5], (HEADS, TOKENS), jnp.float32) ** block_scale(part_keys[5], (HEADS, TOKENS), ((0, 4), (1, 16)), -0.2, 0.2), 6.0, 8.0)
    beacon_keys = gaussian(part_keys[6], (BEACONS, HEADS * HD), 1.0, 6.0, ((0, 16), (1, 4)))
    beacon_values = gaussian(part_keys[7], (BEACONS, HEADS * HD), 1.0, 6.0, ((0, 16), (1, 4)))
    beacon_reach = with_ends(jax.random.randint(part_keys[8], (GROUPS,), 1, GROUPS + 1), jax.random.fold_in(part_keys[8], 1), 1, GROUPS).astype(jnp.int32)
    return {"queries": queries, "keys": keys, "values": values, "out_grad": out_grad, "forward_out": forward_out, "log_norm": log_norm, "beacon_keys": beacon_keys, "beacon_values": beacon_values, "beacon_reach": beacon_reach}


def reference(queries, keys, values, out_grad, forward_out, log_norm, beacon_keys, beacon_values, beacon_reach):
    scaling = 1.0 / math.sqrt(HD)
    token_count = queries.shape[0]
    beacon_count = beacon_keys.shape[0]
    head_count = log_norm.shape[0]

    def by_head(array):
        return array.reshape(array.shape[0], head_count, HD).transpose(1, 0, 2)
    row_group = jnp.arange(token_count, dtype=jnp.int32) // GROUP
    row_reach = beacon_reach[row_group]
    col_group = jnp.arange(beacon_count, dtype=jnp.int32) // BPC
    allowed = (col_group[None, :] <= row_group[:, None]) & (col_group[None, :] > (row_group - row_reach)[:, None])
    causal = jnp.arange(GROUP)[:, None] >= jnp.arange(GROUP)[None, :]

    def one_head(items):
        query_h, key_h, value_h, grad_h, output_h, norm_h, bkey_h, bvalue_h = items
        delta = lax.optimization_barrier(jnp.sum(grad_h.astype(jnp.float32) * output_h.astype(jnp.float32), axis=1))
        scores = jnp.dot(query_h, bkey_h.T, preferred_element_type=jnp.float32) * scaling
        probs = jnp.where(allowed, jnp.exp(scores - norm_h[:, None]), 0.0)
        dprobs = jnp.dot(grad_h, bvalue_h.T, preferred_element_type=jnp.float32)
        dscores = (probs * (dprobs - delta[:, None])).astype(jnp.bfloat16)
        weights = probs.astype(jnp.bfloat16)
        query_beacon = jnp.dot(dscores, bkey_h, preferred_element_type=jnp.float32) * scaling
        bkey_grad = jnp.dot(dscores.T, query_h, preferred_element_type=jnp.float32) * scaling
        bvalue_grad = jnp.dot(weights.T, grad_h, preferred_element_type=jnp.float32)
        query4 = query_h.reshape(GROUPS, GROUP, HD).astype(jnp.float32)
        key4 = key_h.reshape(GROUPS, GROUP, HD).astype(jnp.float32)
        value4 = value_h.reshape(GROUPS, GROUP, HD).astype(jnp.float32)
        grad4 = grad_h.reshape(GROUPS, GROUP, HD).astype(jnp.float32)
        norm4 = norm_h.reshape(GROUPS, GROUP)
        delta4 = delta.reshape(GROUPS, GROUP)
        raw_scores = jnp.einsum('cqd,ckd->cqk', query4, key4) * scaling
        raw_probs = jnp.where(causal[None], jnp.exp(raw_scores - norm4[:, :, None]), 0.0)
        raw_dprobs = jnp.einsum('cqd,ckd->cqk', grad4, value4)
        raw_ds = (raw_probs * (raw_dprobs - delta4[:, :, None])).astype(jnp.bfloat16)
        raw_ds = lax.optimization_barrier(raw_ds).astype(jnp.float32)
        raw_weights = raw_probs.astype(jnp.bfloat16)
        raw_weights = lax.optimization_barrier(raw_weights).astype(jnp.float32)
        query_raw = jnp.einsum('cqk,ckd->cqd', raw_ds, key4) * scaling
        key_raw = jnp.einsum('cqk,cqd->ckd', raw_ds, query4) * scaling
        value_raw = jnp.einsum('cqk,cqd->ckd', raw_weights, grad4)
        query_total = query_beacon + query_raw.reshape(token_count, HD)
        return (query_total, key_raw.reshape(token_count, HD), value_raw.reshape(token_count, HD), bkey_grad, bvalue_grad)
    results = lax.map(one_head, (by_head(queries), by_head(keys), by_head(values), by_head(out_grad), by_head(forward_out), log_norm, by_head(beacon_keys), by_head(beacon_values)))

    def back(array):
        return array.transpose(1, 0, 2).reshape(array.shape[1], head_count * HD).astype(jnp.bfloat16)
    return (back(results[0]), back(results[1]), back(results[2]), back(results[3]), back(results[4]))
```

```python
import functools
import math

import jax
import jax.numpy as jnp
from jax import lax
from jax.experimental import pallas as pl
from jax.experimental.pallas import tpu as pltpu
from jax.sharding import PartitionSpec as P

HD = 128
GROUP = 512
BPC = 64
CHIPS = 8
SCALE = 1.0 / math.sqrt(HD)
LOG2E = math.log2(math.e)
HIDDEN = 1e30
BF = jnp.bfloat16
F32 = jnp.float32


def nt(a, b):
    return lax.dot_general(a, b, (((1,), (1,)), ((), ())), preferred_element_type=F32)


def nn(a, b):
    return lax.dot_general(a, b, (((1,), (0,)), ((), ())), preferred_element_type=F32)


def tn(a, b):
    return lax.dot_general(a, b, (((0,), (0,)), ((), ())), preferred_element_type=F32)


def raw_kernel(place, q_ref, k_ref, v_ref, g_ref, o_ref, ln_ref, dq_ref, dk_ref, dv_ref, st_ref):
    h = pl.program_id(0)
    q, k, v, g = q_ref[...], k_ref[...], v_ref[...], g_ref[...]
    prod = g.astype(F32) * o_ref[...].astype(F32)
    delta = jnp.sum(prod.T, axis=0, keepdims=True)
    ln = ln_ref[pl.ds(h, 1), :] * LOG2E
    st_ref[0, pl.ds(h, 1), :] = ln
    st_ref[1, pl.ds(h, 1), :] = delta
    st_ref[2, pl.ds(h, 1), :] = jnp.full((1, GROUP), place[2], jnp.int32).astype(F32)
    block = 128
    tri = lax.broadcasted_iota(jnp.int32, (block, block), 0) <= lax.broadcasted_iota(
        jnp.int32, (block, block), 1
    )
    stripes = []
    for lo in range(0, GROUP, block):
        hi = lo + block
        s = nt(k[lo:hi], q[lo:])
        p = jnp.exp2(s * (SCALE * LOG2E) - ln[:, lo:])
        head = jnp.where(tri, p[:, :block], 0.0)
        p = head if hi == GROUP else jnp.concatenate([head, p[:, block:]], axis=1)
        dp = nt(v[lo:hi], g[lo:])
        ds = (p * (dp - delta[:, lo:])).astype(BF)
        dv_ref[lo:hi, :] = nn(p.astype(BF), g[lo:]).astype(BF)
        dk_ref[lo:hi, :] = (nn(ds, q[lo:]) * SCALE).astype(BF)
        stripes.append(ds)
    for lo in range(0, GROUP, block):
        hi = lo + block
        parts = [stripe[:, lo - i * block : hi - i * block] for i, stripe in enumerate(stripes[: hi // block])]
        ds = parts[0] if len(parts) == 1 else jnp.concatenate(parts, axis=0)
        dq_ref[lo:hi, :] = tn(ds, k[:hi]) * SCALE


def raw_call(place, queries, keys, values, out_grad, forward_out, log_norm):
    heads = log_norm.shape[0]
    column = pl.BlockSpec((GROUP, HD), lambda h: (0, h))
    whole = pl.BlockSpec((heads, GROUP), lambda h: (0, 0))
    width = heads * HD
    return pl.pallas_call(
        raw_kernel,
        grid=(heads,),
        in_specs=[pl.BlockSpec(memory_space=pltpu.SMEM)] + [column] * 5 + [whole],
        out_specs=[column] * 3 + [pl.BlockSpec((3, heads, GROUP), lambda h: (0, 0, 0))],
        out_shape=[
            jax.ShapeDtypeStruct((GROUP, width), F32),
            jax.ShapeDtypeStruct((GROUP, width), BF),
            jax.ShapeDtypeStruct((GROUP, width), BF),
            jax.ShapeDtypeStruct((3, heads, GROUP), F32),
        ],
        compiler_params=pltpu.CompilerParams(vmem_limit_bytes=48 << 20),
        cost_estimate=pl.CostEstimate(
            flops=10 * heads * GROUP * GROUP * HD, bytes_accessed=10 << 20, transcendentals=heads * GROUP * GROUP
        ),
        name="raw_tokens",
    )(place, queries, keys, values, out_grad, forward_out, log_norm)


def beacon_kernel(step, count, place, qh_ref, qp_ref, gh_ref, gp_ref, sh_ref, sp_ref, *refs):
    pieces, outs, ds_ref = refs[:count], refs[count : 2 * count], refs[2 * count]
    h = pl.program_id(0)
    z, core = place[0], place[1]
    chunk = jnp.where(core == 0, z - step, z + step - CHIPS) if step else z
    valid = (chunk >= 0) & ((core == 0) | (step < CHIPS // 2))
    owners = [2 * chunk + core, 2 * chunk + 1 - core][:count]

    def work():
        kk = pieces[0][0] if count == 1 else jnp.concatenate([ref[0] for ref in pieces], axis=0)
        vv = pieces[0][1] if count == 1 else jnp.concatenate([ref[1] for ref in pieces], axis=0)
        dk = dv = None
        for side, (q_ref, g_ref, st_ref, group) in enumerate(
            ((qh_ref, gh_ref, sh_ref, 2 * z + core), (qp_ref, gp_ref, sp_ref, 2 * z + 1 - core))
        ):
            q, g = q_ref[...], g_ref[...]
            ln, delta = st_ref[0, pl.ds(h, 1), :], st_ref[1, pl.ds(h, 1), :]
            reach = st_ref[2, pl.ds(h, 1), :]
            rows = []
            for owner in owners:
                far = jnp.where(owner <= group, group - owner, 2 * CHIPS)
                row = jnp.where(reach > jnp.full((1, GROUP), far, jnp.int32).astype(F32), ln, HIDDEN)
                rows.append(jnp.broadcast_to(row, (BPC, GROUP)))
            bias = rows[0] if count == 1 else jnp.concatenate(rows, axis=0)
            p = jnp.exp2(nt(kk, q) * (SCALE * LOG2E) - bias)
            ds = (p * (nt(vv, g) - delta)).astype(BF)
            ds_ref[0, :, side * GROUP : (side + 1) * GROUP] = ds
            dv_part, dk_part = nn(p.astype(BF), g), nn(ds, q)
            dk, dv = (dk_part, dv_part) if dk is None else (dk + dk_part, dv + dv_part)
        dk = dk * SCALE
        for i, ref in enumerate(outs):
            ref[0] = dk[i * BPC : (i + 1) * BPC].astype(ref.dtype)
            ref[1] = dv[i * BPC : (i + 1) * BPC].astype(ref.dtype)

    if step == 0:
        work()
        return
    pl.when(valid)(work)

    @pl.when(jnp.logical_not(valid))
    def _():
        for ref in outs:
            ref[...] = jnp.zeros_like(ref)
        ds_ref[...] = jnp.zeros_like(ds_ref)


def beacon_call(step, place, sides, pieces, kind):
    heads = sides[4].shape[1]
    count = len(pieces)
    column = pl.BlockSpec((GROUP, HD), lambda h: (0, h))
    stats = pl.BlockSpec((3, heads, GROUP), lambda h: (0, 0, 0))
    piece = pl.BlockSpec((2, BPC, HD), lambda h: (0, 0, h))
    items = heads * 2 * GROUP * count * BPC
    return pl.pallas_call(
        functools.partial(beacon_kernel, step, count),
        grid=(heads,),
        in_specs=[pl.BlockSpec(memory_space=pltpu.SMEM)] + [column] * 4 + [stats] * 2 + [piece] * count,
        out_specs=[piece] * count + [pl.BlockSpec((1, count * BPC, 2 * GROUP), lambda h: (h, 0, 0))],
        out_shape=[jax.ShapeDtypeStruct((2, BPC, heads * HD), kind)] * count
        + [jax.ShapeDtypeStruct((heads, count * BPC, 2 * GROUP), BF)],
        compiler_params=pltpu.CompilerParams(vmem_limit_bytes=48 << 20),
        cost_estimate=pl.CostEstimate(flops=8 * items * HD, bytes_accessed=8 << 20, transcendentals=items),
        name="beacon_step" + str(step),
    )(place, *sides, *pieces)


def query_kernel(steps, raw_ref, *refs):
    ds_refs, k_refs, (home_ref, other_ref) = refs[:steps], refs[steps:-2], refs[-2:]
    kk = jnp.concatenate([ref[0] for ref in k_refs], axis=0)
    home = jnp.concatenate([ref[0, :, :GROUP] for ref in ds_refs], axis=0)
    home_ref[...] = raw_ref[...] + tn(home, kk) * SCALE
    other = jnp.concatenate([ref[0, :, GROUP:] for ref in ds_refs], axis=0)
    other_ref[...] = tn(other, kk) * SCALE


def query_call(raw, ds_list, pieces):
    heads = ds_list[0].shape[0]
    column = pl.BlockSpec((GROUP, HD), lambda h: (0, h))
    piece = pl.BlockSpec((1, BPC, HD), lambda h: (0, 0, h))
    rows = sum(ds.shape[1] for ds in ds_list)
    return pl.pallas_call(
        functools.partial(query_kernel, len(ds_list)),
        grid=(heads,),
        in_specs=[column]
        + [pl.BlockSpec((1, ds.shape[1], 2 * GROUP), lambda h: (h, 0, 0)) for ds in ds_list]
        + [piece] * len(pieces),
        out_specs=[column] * 2,
        out_shape=[jax.ShapeDtypeStruct((GROUP, heads * HD), F32)] * 2,
        compiler_params=pltpu.CompilerParams(vmem_limit_bytes=48 << 20),
        cost_estimate=pl.CostEstimate(
            flops=2 * heads * rows * 2 * GROUP * HD, bytes_accessed=16 << 20, transcendentals=0
        ),
        name="query_grad",
    )(raw, *ds_list, *pieces)


def at(z, core):
    return 2 * (z % CHIPS) + core


SWAP = [(at(z, core), at(z, 1 - core)) for z in range(CHIPS) for core in (0, 1)]


def gather_pairs(cross):
    pairs = []
    for z in range(CHIPS):
        pairs.append((at(z, 1 if cross else 0), at(z + 1, 0)))
        pairs.append((at(z, 0 if cross else 1), at(z - 1, 1)))
    return pairs


def reduce_pairs(cross):
    pairs = []
    for z in range(CHIPS):
        pairs.append((at(z, 0), at(z - 1, 1 if cross else 0)))
        pairs.append((at(z, 1), at(z + 1, 0 if cross else 1)))
    return pairs


def local(
    queries, keys, values, out_grad, forward_out, log_norm, beacon_keys, beacon_values, beacon_reach
):
    ctx = lax.axis_index("ctx").astype(jnp.int32)
    place = jnp.stack([ctx // 2, ctx % 2, beacon_reach[0].astype(jnp.int32)])
    own = jnp.stack([beacon_keys, beacon_values])
    hops = [
        (lax.ppermute(own, "ctx", gather_pairs(False)), lax.ppermute(own, "ctx", gather_pairs(True)))
    ]
    queries_other = lax.ppermute(queries, "ctx", SWAP)
    grad_other = lax.ppermute(out_grad, "ctx", SWAP)
    dq_raw, key_grad, value_grad, stats = raw_call(
        place, queries, keys, values, out_grad, forward_out, log_norm
    )
    stats_other = lax.ppermute(stats, "ctx", SWAP)
    sides = (queries, queries_other, out_grad, grad_other, stats, stats_other)
    for _ in range(CHIPS // 2 - 1):
        hops.append(tuple(lax.ppermute(piece, "ctx", gather_pairs(False)) for piece in hops[-1]))
    own_term, own_ds = beacon_call(0, place, sides, (own,), F32)
    terms, ds_list, pieces = [], [own_ds], [own]
    for step, arrived in enumerate(hops, 1):
        kind = BF if step == len(hops) else F32
        term_a, term_b, ds = beacon_call(step, place, sides, arrived, kind)
        terms.append((term_a, term_b))
        ds_list.append(ds)
        pieces.extend(arrived)
    carried = terms[-1]
    for hop in range(len(hops) - 1, 0, -1):
        carried = tuple(lax.ppermute(piece, "ctx", reduce_pairs(False)) for piece in carried)
        carried = tuple(
            (piece.astype(F32) + term).astype(BF) for piece, term in zip(carried, terms[hop - 1], strict=True)
        )
    end_a = lax.ppermute(carried[0], "ctx", reduce_pairs(False))
    end_b = lax.ppermute(carried[1], "ctx", reduce_pairs(True))
    total = (own_term + (end_a.astype(F32) + end_b.astype(F32))).astype(BF)
    dq_home, dq_other = query_call(dq_raw, ds_list, pieces)
    query_grad = (dq_home + lax.ppermute(dq_other, "ctx", SWAP)).astype(BF)
    return query_grad, key_grad, value_grad, total[0], total[1]


def solution(mesh):
    tokens = P(("dp", "ctx"), "head")
    in_specs = (tokens,) * 5 + (P("head", ("dp", "ctx")), tokens, tokens, P(("dp", "ctx")))
    return jax.shard_map(local, mesh=mesh, in_specs=in_specs, out_specs=(tokens,) * 5, check_vma=False)
```

```python
import functools
import math

import jax
import jax.numpy as jnp
from jax import lax
from jax.experimental import pallas as pl
from jax.experimental.pallas import tpu as pltpu
from jax.sharding import PartitionSpec as P

HD = 128
GROUP = 512
BPC = 64
CHIPS = 8
SCALE = 1.0 / math.sqrt(HD)
LOG2E = math.log2(math.e)
HIDDEN = 1e30
BF = jnp.bfloat16
F32 = jnp.float32


def nt(a, b):
    return lax.dot_general(a, b, (((1,), (1,)), ((), ())), preferred_element_type=F32)


def nn(a, b):
    return lax.dot_general(a, b, (((1,), (0,)), ((), ())), preferred_element_type=F32)


def tn(a, b):
    return lax.dot_general(a, b, (((0,), (0,)), ((), ())), preferred_element_type=F32)


def stats_kernel(
    place, q_any, k_any, v_any, g_any, o_any, ln_any,
    q_ref, k_ref, v_ref, g_ref, st_ref, o_ref, ln_ref, sems,
):
    pairs = ((g_any, g_ref), (o_any, o_ref), (ln_any, ln_ref), (q_any, q_ref), (k_any, k_ref), (v_any, v_ref))
    copies = [pltpu.make_async_copy(src, dst, sems.at[i]) for i, (src, dst) in enumerate(pairs)]
    for copy in copies:
        copy.start()
    st_ref[2] = jnp.full(st_ref.shape[1:], place[2], jnp.int32).astype(F32)
    for copy in copies[:3]:
        copy.wait()
    st_ref[0] = ln_ref[...] * LOG2E
    for h in range(ln_ref.shape[0]):
        c = slice(h * HD, (h + 1) * HD)
        prod = g_ref[:, c].astype(F32) * o_ref[:, c].astype(F32)
        st_ref[1, h : h + 1, :] = jnp.sum(prod.T, axis=0, keepdims=True)
    for copy in copies[3:]:
        copy.wait()


def raw_kernel(q_ref, k_ref, v_ref, g_ref, st_ref, wait, dq_ref, dk_ref, dv_ref):
    block = 256
    tri = lax.broadcasted_iota(jnp.int32, (block, block), 0) <= lax.broadcasted_iota(
        jnp.int32, (block, block), 1
    )
    for h in range(st_ref.shape[1]):
        c = slice(h * HD, (h + 1) * HD)
        q, k, v, g = q_ref[:, c], k_ref[:, c], v_ref[:, c], g_ref[:, c]
        ln, delta = st_ref[0, h : h + 1, :], st_ref[1, h : h + 1, :]
        stripes = []
        for lo in range(0, GROUP, block):
            hi = lo + block
            p = jnp.exp2(nt(k[lo:hi], q[lo:]) * (SCALE * LOG2E) - ln[:, lo:])
            head = jnp.where(tri, p[:, :block], 0.0)
            p = head if hi == GROUP else jnp.concatenate([head, p[:, block:]], axis=1)
            ds = (p * (nt(v[lo:hi], g[lo:]) - delta[:, lo:])).astype(BF)
            dv_ref[lo:hi, c] = nn(p.astype(BF), g[lo:]).astype(BF)
            dk_ref[lo:hi, c] = (nn(ds, q[lo:]) * SCALE).astype(BF)
            stripes.append(ds)
        for lo in range(0, GROUP, block):
            hi = lo + block
            parts = [part[:, lo - i * block : hi - i * block] for i, part in enumerate(stripes[: hi // block])]
            ds = parts[0] if len(parts) == 1 else jnp.concatenate(parts, axis=0)
            dq_ref[lo:hi, c] = (tn(k[:hi], ds) * SCALE).T


SMEM = pl.BlockSpec(memory_space=pltpu.SMEM)
VMEM = pl.BlockSpec(memory_space=pltpu.VMEM)
ANY = pl.BlockSpec(memory_space=pl.ANY)


def stats_call(place, arrays):
    heads = arrays[-1].shape[0]
    wide = (GROUP, heads * HD)
    return pl.pallas_call(
        stats_kernel,
        in_specs=[SMEM] + [ANY] * 6,
        out_specs=[VMEM] * 5,
        out_shape=[jax.ShapeDtypeStruct(wide, BF)] * 4
        + [jax.ShapeDtypeStruct((3, heads, GROUP), F32)],
        scratch_shapes=[
            pltpu.VMEM(wide, BF),
            pltpu.VMEM((heads, GROUP), F32),
            pltpu.SemaphoreType.DMA((6,)),
        ],
        compiler_params=pltpu.CompilerParams(vmem_limit_bytes=16 << 20),
        cost_estimate=pl.CostEstimate(
            flops=2 * heads * GROUP * HD, bytes_accessed=8 << 20, transcendentals=0
        ),
        name="stats",
    )(place, *[pltpu.with_memory_space_constraint(x, pltpu.HBM) for x in arrays])


def raw_call(queries, keys, values, out_grad, stats, wait):
    heads = stats.shape[1]
    wide = queries.shape
    return pl.pallas_call(
        raw_kernel,
        in_specs=[VMEM] * 5 + [ANY],
        out_specs=[VMEM] * 3,
        out_shape=[jax.ShapeDtypeStruct(wide, kind) for kind in (F32, BF, BF)],
        compiler_params=pltpu.CompilerParams(vmem_limit_bytes=16 << 20),
        cost_estimate=pl.CostEstimate(
            flops=10 * heads * GROUP * GROUP * HD, bytes_accessed=10 << 20, transcendentals=heads * GROUP * GROUP
        ),
        name="raw_tokens",
    )(queries, keys, values, out_grad, stats, wait)


def beacon_kernel(shifts, waits, place, qh_ref, qp_ref, gh_ref, gp_ref, sh_ref, sp_ref, *refs):
    count = len(shifts)
    pieces, refs = refs[:count], refs[count + waits :]
    outs, ds_ref = refs[:count], refs[count]
    z, core = place[0], place[1]
    chunks = [z + shift for shift in shifts]
    sides = ((qh_ref, gh_ref, sh_ref, 2 * z + core), (qp_ref, gp_ref, sp_ref, 2 * z + 1 - core))

    def work():
        far = [
            [
                jnp.where((chunk >= 0) & (2 * chunk + core <= group), group - 2 * chunk - core, 2 * CHIPS)
                for chunk in chunks
            ]
            for *_, group in sides
        ]
        for h in range(sh_ref.shape[1]):
            c = slice(h * HD, (h + 1) * HD)
            kk = jnp.concatenate([ref[0, :, c] for ref in pieces], axis=0)
            vv = jnp.concatenate([ref[1, :, c] for ref in pieces], axis=0)
            dk = dv = None
            for side, (q_ref, g_ref, st_ref, _) in enumerate(sides):
                q, g = q_ref[:, c], g_ref[:, c]
                ln, delta, reach = (st_ref[i, h : h + 1, :] for i in range(3))
                bias = jnp.concatenate(
                    [
                        jnp.broadcast_to(
                            jnp.where(reach > jnp.full((1, GROUP), d, jnp.int32).astype(F32), ln, HIDDEN),
                            (BPC, GROUP),
                        )
                        for d in far[side]
                    ],
                    axis=0,
                )
                p = jnp.exp2(nt(kk, q) * (SCALE * LOG2E) - bias)
                ds = (p * (nt(vv, g) - delta)).astype(BF)
                ds_ref[h, :, side * GROUP : (side + 1) * GROUP] = ds
                dv_part, dk_part = nn(p.astype(BF), g), nn(ds, q)
                dk, dv = (dk_part, dv_part) if dk is None else (dk + dk_part, dv + dv_part)
            dk = dk * SCALE
            for i, ref in enumerate(outs):
                ref[0, :, c] = dk[i * BPC : (i + 1) * BPC].astype(ref.dtype)
                ref[1, :, c] = dv[i * BPC : (i + 1) * BPC].astype(ref.dtype)

    if 0 in shifts:
        work()
        return
    valid = functools.reduce(jnp.logical_or, [chunk >= 0 for chunk in chunks])
    pl.when(valid)(work)

    @pl.when(jnp.logical_not(valid))
    def _():
        for ref in outs:
            ref[...] = jnp.zeros_like(ref)
        ds_ref[...] = jnp.zeros_like(ds_ref)


def beacon_call(place, sides, parts, waits, name):
    pieces, shifts, kinds = zip(*parts, strict=True)
    heads = sides[4].shape[1]
    count = len(pieces)
    items = heads * 2 * GROUP * count * BPC
    return pl.pallas_call(
        functools.partial(beacon_kernel, shifts, len(waits)),
        in_specs=[SMEM] + [VMEM] * (6 + count) + [ANY] * len(waits),
        out_specs=[VMEM] * (count + 1),
        out_shape=[jax.ShapeDtypeStruct((2, BPC, heads * HD), kind) for kind in kinds]
        + [jax.ShapeDtypeStruct((heads, count * BPC, 2 * GROUP), BF)],
        compiler_params=pltpu.CompilerParams(vmem_limit_bytes=16 << 20),
        cost_estimate=pl.CostEstimate(flops=8 * items * HD, bytes_accessed=8 << 20, transcendentals=items),
        name=name,
    )(place, *sides, *pieces, *waits)


def query_kernel(steps, *refs):
    ds_refs, k_refs, outs = refs[:steps], refs[steps:-2], refs[-2:]
    for h in range(ds_refs[0].shape[0]):
        c = slice(h * HD, (h + 1) * HD)
        kk = jnp.concatenate([ref[0, :, c] for ref in k_refs], axis=0)
        for side, out in enumerate(outs):
            ds = jnp.concatenate([ref[h, :, side * GROUP : (side + 1) * GROUP] for ref in ds_refs], axis=0)
            out[:, c] = (tn(kk, ds) * SCALE).T.astype(out.dtype)


def query_call(ds_list, pieces):
    heads = ds_list[0].shape[0]
    rows = sum(ds.shape[1] for ds in ds_list)
    return pl.pallas_call(
        functools.partial(query_kernel, len(ds_list)),
        in_specs=[VMEM] * (len(ds_list) + len(pieces)),
        out_specs=[VMEM] * 2,
        out_shape=[jax.ShapeDtypeStruct((GROUP, heads * HD), kind) for kind in (F32, BF)],
        compiler_params=pltpu.CompilerParams(vmem_limit_bytes=16 << 20),
        cost_estimate=pl.CostEstimate(
            flops=2 * heads * rows * 2 * GROUP * HD, bytes_accessed=16 << 20, transcendentals=0
        ),
        name="query_grad",
    )(*ds_list, *pieces)


def join(array, *after):
    return pl.pallas_call(
        lambda *refs: None,
        in_specs=[ANY] * (1 + len(after)),
        out_specs=ANY,
        out_shape=jax.ShapeDtypeStruct(array.shape, array.dtype),
        input_output_aliases={0: 0},
        compiler_params=pltpu.CompilerParams(vmem_limit_bytes=1 << 20),
        name="join",
    )(array, *after)


def both(a, b, *after):
    a = join(a, b, *after)
    return a, join(b, a)


def at(z, core):
    return 2 * (z % CHIPS) + core


SWAP = [(at(z, core), at(z, 1 - core)) for z in range(CHIPS) for core in (0, 1)]


UP = [(at(z, core), at(z + 1, core)) for z in range(CHIPS) for core in (0, 1)]
FAR = [(at(z, core), at(z + 4, core)) for z in range(CHIPS - 4) for core in (0, 1)]
DOWN = [(at(z, core), at(z - 1, core)) for z in range(CHIPS) for core in (0, 1)]


def local(
    queries, keys, values, out_grad, forward_out, log_norm, beacon_keys, beacon_values, beacon_reach
):
    ctx = lax.axis_index("ctx").astype(jnp.int32)
    place = jnp.stack([ctx // 2, ctx % 2, beacon_reach[0].astype(jnp.int32)])
    send = functools.partial(lax.ppermute, axis_name="ctx")
    own = jnp.stack([beacon_keys, beacon_values])
    a1, b1, d4 = send(own, perm=UP), send(own, perm=DOWN), send(own, perm=FAR)
    queries_other, grad_other = send(queries, perm=SWAP), send(out_grad, perm=SWAP)
    q_home, k_home, v_home, g_home, stats = stats_call(
        place, (queries, keys, values, out_grad, forward_out, log_norm)
    )
    sides = (q_home, queries_other, g_home, grad_other, stats, send(stats, perm=SWAP))
    a1, b1 = both(a1, b1, stats)
    a2, b2 = send(a1, perm=UP), send(b1, perm=DOWN)
    t1a, t1b, t0, ds1 = beacon_call(
        place, sides, ((a1, -1, F32), (b1, 1 - CHIPS, F32), (own, 0, F32)), (), "beacons_near"
    )
    a2, b2 = both(a2, b2, ds1)
    a3, b3 = send(a2, perm=UP), send(b2, perm=DOWN)
    t4, ds4 = beacon_call(place, sides, ((d4, -4, BF),), (a2, b2), "beacons_far")
    a3, b3 = both(a3, b3, t4)

    def plus(arrived, term):
        return (arrived.astype(F32) + term).astype(BF)

    a = send(t4, perm=DOWN)
    t3a, b, ds3 = beacon_call(place, sides, ((a3, -3, F32), (b3, 3 - CHIPS, BF)), (t4,), "beacons_third")
    a, b = both(a, b)
    a, b = send(plus(a, t3a), perm=DOWN), send(b, perm=UP)
    t2a, t2b, ds2 = beacon_call(
        place, sides, ((a2, -2, F32), (b2, 2 - CHIPS, F32)), (t3a,), "beacons_second"
    )
    a, b = both(a, b, ds2)
    a, b = send(plus(a, t2a), perm=DOWN), send(plus(b, t2b), perm=UP)
    dq_home, dq_other = query_call((ds1, ds2, ds3, ds4), (a1, b1, own, a2, b2, a3, b3, d4))
    a, b = both(a, b, dq_other)
    a, b = send(plus(a, t1a), perm=DOWN), send(plus(b, t1b), perm=UP)
    dq_raw, key_grad, value_grad = raw_call(q_home, k_home, v_home, g_home, stats, dq_other)
    query_grad = (dq_raw + dq_home + send(dq_other, perm=SWAP).astype(F32)).astype(BF)
    total = (join(t0, query_grad) + (a.astype(F32) + b.astype(F32))).astype(BF)
    return query_grad, key_grad, value_grad, total[0], total[1]


def solution(mesh):
    tokens = P(("dp", "ctx"), "head")
    in_specs = (tokens,) * 5 + (P("head", ("dp", "ctx")), tokens, tokens, P(("dp", "ctx")))
    return jax.shard_map(local, mesh=mesh, in_specs=in_specs, out_specs=(tokens,) * 5, check_vma=False)
```

```python
import functools
import math

import jax
import jax.numpy as jnp
from jax import lax
from jax.experimental import pallas as pl
from jax.experimental.pallas import tpu as pltpu
from jax.sharding import PartitionSpec as P

HD = 128
GROUP = 512
BPC = 64
CHIPS = 8
SCALE = 1.0 / math.sqrt(HD)
LOG2E = math.log2(math.e)
HIDDEN = 1e30
BF = jnp.bfloat16
F32 = jnp.float32


def nt(a, b):
    return lax.dot_general(a, b, (((1,), (1,)), ((), ())), preferred_element_type=F32)


def nn(a, b):
    return lax.dot_general(a, b, (((1,), (0,)), ((), ())), preferred_element_type=F32)


def tn(a, b):
    return lax.dot_general(a, b, (((0,), (0,)), ((), ())), preferred_element_type=F32)


def stats_kernel(
    place, q_any, k_any, v_any, g_any, o_any, ln_any,
    q_ref, k_ref, v_ref, g_ref, st_ref, o_ref, ln_ref, sems,
):
    pairs = ((g_any, g_ref), (o_any, o_ref), (ln_any, ln_ref), (q_any, q_ref), (k_any, k_ref), (v_any, v_ref))
    copies = [pltpu.make_async_copy(src, dst, sems.at[i]) for i, (src, dst) in enumerate(pairs)]
    for copy in copies:
        copy.start()
    st_ref[2] = jnp.full(st_ref.shape[1:], place[2], jnp.int32).astype(F32)
    for copy in copies[:3]:
        copy.wait()
    st_ref[0] = ln_ref[...] * LOG2E
    for h in range(ln_ref.shape[0]):
        c = slice(h * HD, (h + 1) * HD)
        prod = g_ref[:, c].astype(F32) * o_ref[:, c].astype(F32)
        st_ref[1, h : h + 1, :] = jnp.sum(prod.T, axis=0, keepdims=True)
    for copy in copies[3:]:
        copy.wait()


def raw_kernel(q_ref, k_ref, v_ref, g_ref, st_ref, wait, dq_ref, dk_ref, dv_ref):
    block = 256
    tri = lax.broadcasted_iota(jnp.int32, (block, block), 0) <= lax.broadcasted_iota(
        jnp.int32, (block, block), 1
    )
    for h in range(st_ref.shape[1]):
        c = slice(h * HD, (h + 1) * HD)
        q, k, v, g = q_ref[:, c], k_ref[:, c], v_ref[:, c], g_ref[:, c]
        ln, delta = st_ref[0, h : h + 1, :], st_ref[1, h : h + 1, :]
        stripes = []
        for lo in range(0, GROUP, block):
            hi = lo + block
            p = jnp.exp2(nt(k[lo:hi], q[lo:]) * (SCALE * LOG2E) - ln[:, lo:])
            head = jnp.where(tri, p[:, :block], 0.0)
            p = head if hi == GROUP else jnp.concatenate([head, p[:, block:]], axis=1)
            ds = (p * (nt(v[lo:hi], g[lo:]) - delta[:, lo:])).astype(BF)
            dv_ref[lo:hi, c] = nn(p.astype(BF), g[lo:]).astype(BF)
            dk_ref[lo:hi, c] = (nn(ds, q[lo:]) * SCALE).astype(BF)
            stripes.append(ds)
        for lo in range(0, GROUP, block):
            hi = lo + block
            parts = [part[:, lo - i * block : hi - i * block] for i, part in enumerate(stripes[: hi // block])]
            ds = parts[0] if len(parts) == 1 else jnp.concatenate(parts, axis=0)
            dq_ref[lo:hi, c] = (tn(k[:hi], ds) * SCALE).T


SMEM = pl.BlockSpec(memory_space=pltpu.SMEM)
VMEM = pl.BlockSpec(memory_space=pltpu.VMEM)
ANY = pl.BlockSpec(memory_space=pl.ANY)


def stats_call(place, arrays):
    heads = arrays[-1].shape[0]
    wide = (GROUP, heads * HD)
    return pl.pallas_call(
        stats_kernel,
        in_specs=[SMEM] + [ANY] * 6,
        out_specs=[VMEM] * 5,
        out_shape=[jax.ShapeDtypeStruct(wide, BF)] * 4
        + [jax.ShapeDtypeStruct((3, heads, GROUP), F32)],
        scratch_shapes=[
            pltpu.VMEM(wide, BF),
            pltpu.VMEM((heads, GROUP), F32),
            pltpu.SemaphoreType.DMA((6,)),
        ],
        compiler_params=pltpu.CompilerParams(vmem_limit_bytes=16 << 20),
        cost_estimate=pl.CostEstimate(
            flops=2 * heads * GROUP * HD, bytes_accessed=8 << 20, transcendentals=0
        ),
        name="stats",
    )(place, *[pltpu.with_memory_space_constraint(x, pltpu.HBM) for x in arrays])


def raw_call(queries, keys, values, out_grad, stats, wait):
    heads = stats.shape[1]
    wide = queries.shape
    return pl.pallas_call(
        raw_kernel,
        in_specs=[VMEM] * 5 + [ANY],
        out_specs=[VMEM] * 3,
        out_shape=[jax.ShapeDtypeStruct(wide, kind) for kind in (F32, BF, BF)],
        compiler_params=pltpu.CompilerParams(vmem_limit_bytes=16 << 20),
        cost_estimate=pl.CostEstimate(
            flops=10 * heads * GROUP * GROUP * HD, bytes_accessed=10 << 20, transcendentals=heads * GROUP * GROUP
        ),
        name="raw_tokens",
    )(queries, keys, values, out_grad, stats, wait)


def beacon_kernel(shifts, waits, place, qh_ref, qp_ref, gh_ref, gp_ref, sh_ref, sp_ref, *refs):
    count = len(shifts)
    pieces, refs = refs[:count], refs[count + waits :]
    outs, ds_ref = refs[:count], refs[count]
    z, core = place[0], place[1]
    chunks = [z + shift for shift in shifts]
    sides = ((qh_ref, gh_ref, sh_ref, 2 * z + core), (qp_ref, gp_ref, sp_ref, 2 * z + 1 - core))

    def work():
        far = [
            [
                jnp.where((chunk >= 0) & (2 * chunk + core <= group), group - 2 * chunk - core, 2 * CHIPS)
                for chunk in chunks
            ]
            for *_, group in sides
        ]
        for h in range(sh_ref.shape[1]):
            c = slice(h * HD, (h + 1) * HD)
            kk = jnp.concatenate([ref[0, :, c] for ref in pieces], axis=0)
            vv = jnp.concatenate([ref[1, :, c] for ref in pieces], axis=0)
            dk = dv = None
            for side, (q_ref, g_ref, st_ref, _) in enumerate(sides):
                q, g = q_ref[:, c], g_ref[:, c]
                ln, delta, reach = (st_ref[i, h : h + 1, :] for i in range(3))
                bias = jnp.concatenate(
                    [
                        jnp.broadcast_to(
                            jnp.where(reach > jnp.full((1, GROUP), d, jnp.int32).astype(F32), ln, HIDDEN),
                            (BPC, GROUP),
                        )
                        for d in far[side]
                    ],
                    axis=0,
                )
                p = jnp.exp2(nt(kk, q) * (SCALE * LOG2E) - bias)
                ds = (p * (nt(vv, g) - delta)).astype(BF)
                ds_ref[h, :, side * GROUP : (side + 1) * GROUP] = ds
                dv_part, dk_part = nn(p.astype(BF), g), nn(ds, q)
                dk, dv = (dk_part, dv_part) if dk is None else (dk + dk_part, dv + dv_part)
            dk = dk * SCALE
            for i, ref in enumerate(outs):
                ref[0, :, c] = dk[i * BPC : (i + 1) * BPC].astype(ref.dtype)
                ref[1, :, c] = dv[i * BPC : (i + 1) * BPC].astype(ref.dtype)

    if 0 in shifts:
        work()
        return
    valid = functools.reduce(jnp.logical_or, [chunk >= 0 for chunk in chunks])
    pl.when(valid)(work)

    @pl.when(jnp.logical_not(valid))
    def _():
        for ref in outs:
            ref[...] = jnp.zeros_like(ref)
        ds_ref[...] = jnp.zeros_like(ds_ref)


def beacon_call(place, sides, parts, waits, name):
    pieces, shifts, kinds = zip(*parts, strict=True)
    heads = sides[4].shape[1]
    count = len(pieces)
    items = heads * 2 * GROUP * count * BPC
    return pl.pallas_call(
        functools.partial(beacon_kernel, shifts, len(waits)),
        in_specs=[SMEM] + [VMEM] * (6 + count) + [ANY] * len(waits),
        out_specs=[VMEM] * (count + 1),
        out_shape=[jax.ShapeDtypeStruct((2, BPC, heads * HD), kind) for kind in kinds]
        + [jax.ShapeDtypeStruct((heads, count * BPC, 2 * GROUP), BF)],
        compiler_params=pltpu.CompilerParams(vmem_limit_bytes=16 << 20),
        cost_estimate=pl.CostEstimate(flops=8 * items * HD, bytes_accessed=8 << 20, transcendentals=items),
        name=name,
    )(place, *sides, *pieces, *waits)


def query_kernel(steps, *refs):
    ds_refs, k_refs, outs = refs[:steps], refs[steps:-2], refs[-2:]
    for h in range(ds_refs[0].shape[0]):
        c = slice(h * HD, (h + 1) * HD)
        kk = jnp.concatenate([ref[0, :, c] for ref in k_refs], axis=0)
        for side, out in enumerate(outs):
            ds = jnp.concatenate([ref[h, :, side * GROUP : (side + 1) * GROUP] for ref in ds_refs], axis=0)
            out[:, c] = (tn(kk, ds) * SCALE).T.astype(out.dtype)


def query_call(ds_list, pieces):
    heads = ds_list[0].shape[0]
    rows = sum(ds.shape[1] for ds in ds_list)
    return pl.pallas_call(
        functools.partial(query_kernel, len(ds_list)),
        in_specs=[VMEM] * (len(ds_list) + len(pieces)),
        out_specs=[VMEM] * 2,
        out_shape=[jax.ShapeDtypeStruct((GROUP, heads * HD), kind) for kind in (F32, BF)],
        compiler_params=pltpu.CompilerParams(vmem_limit_bytes=16 << 20),
        cost_estimate=pl.CostEstimate(
            flops=2 * heads * rows * 2 * GROUP * HD, bytes_accessed=16 << 20, transcendentals=0
        ),
        name="query_grad",
    )(*ds_list, *pieces)


def join(array, *after):
    return pl.pallas_call(
        lambda *refs: None,
        in_specs=[ANY] * (1 + len(after)),
        out_specs=ANY,
        out_shape=jax.ShapeDtypeStruct(array.shape, array.dtype),
        input_output_aliases={0: 0},
        compiler_params=pltpu.CompilerParams(vmem_limit_bytes=1 << 20),
        name="join",
    )(array, *after)


def both(a, b, *after):
    a = join(a, b, *after)
    return a, join(b, a)


def at(z, core):
    return 2 * (z % CHIPS) + core


SWAP = [(at(z, core), at(z, 1 - core)) for z in range(CHIPS) for core in (0, 1)]


UP = [(at(z, core), at(z + 1, core)) for z in range(CHIPS) for core in (0, 1)]
DOWN = [(at(z, core), at(z - 1, core)) for z in range(CHIPS) for core in (0, 1)]


def local(
    queries, keys, values, out_grad, forward_out, log_norm, beacon_keys, beacon_values, beacon_reach
):
    ctx = lax.axis_index("ctx").astype(jnp.int32)
    place = jnp.stack([ctx // 2, ctx % 2, beacon_reach[0].astype(jnp.int32)])
    send = functools.partial(lax.ppermute, axis_name="ctx")
    own = jnp.stack([beacon_keys, beacon_values])
    a1, b1 = send(own, perm=UP), send(own, perm=DOWN)
    queries_other, grad_other = send(queries, perm=SWAP), send(out_grad, perm=SWAP)
    q_home, k_home, v_home, g_home, stats = stats_call(
        place, (queries, keys, values, out_grad, forward_out, log_norm)
    )
    sides = (q_home, queries_other, g_home, grad_other, stats, send(stats, perm=SWAP))
    a1, b1 = both(a1, b1, sides[5])
    a2, b2 = send(a1, perm=UP), send(b1, perm=DOWN)
    t1a, t1b, t0, ds1 = beacon_call(
        place, sides, ((a1, -1, F32), (b1, 1 - CHIPS, F32), (own, 0, F32)), (), "beacons_near"
    )
    a2, b2 = both(a2, b2, ds1)
    a3, b3 = send(a2, perm=UP), send(b2, perm=DOWN)
    t2a, t2b, ds2 = beacon_call(place, sides, ((a2, -2, F32), (b2, 2 - CHIPS, F32)), (), "beacons_second")
    a3, b3 = both(a3, b3, ds2)
    a4 = send(a3, perm=UP)
    t4, ds4 = beacon_call(place, sides, ((a4, -4, BF),), (), "beacons_far")

    def plus(arrived, term):
        return (arrived.astype(F32) + term).astype(BF)

    a = send(t4, perm=DOWN)
    t3a, b, ds3 = beacon_call(place, sides, ((a3, -3, F32), (b3, 3 - CHIPS, BF)), (t4,), "beacons_third")
    dq_home, dq_other = query_call((ds1, ds2, ds3, ds4), (a1, b1, own, a2, b2, a3, b3, a4))
    a, b = both(a, b, dq_other)
    a, b = send(plus(a, t3a), perm=DOWN), send(b, perm=UP)
    dq_raw, key_grad, value_grad = raw_call(q_home, k_home, v_home, g_home, stats, dq_other)
    a, b = both(a, b, dq_raw)
    a, b = send(plus(a, t2a), perm=DOWN), send(plus(b, t2b), perm=UP)
    query_grad = (dq_raw + dq_home + send(dq_other, perm=SWAP).astype(F32)).astype(BF)
    a, b = both(a, b, query_grad)
    a, b = send(plus(a, t1a), perm=DOWN), send(plus(b, t1b), perm=UP)
    total = (t0 + (a.astype(F32) + b.astype(F32))).astype(BF)
    return query_grad, key_grad, value_grad, total[0], total[1]


def solution(mesh):
    tokens = P(("dp", "ctx"), "head")
    in_specs = (tokens,) * 5 + (P("head", ("dp", "ctx")), tokens, tokens, P(("dp", "ctx")))
    return jax.shard_map(local, mesh=mesh, in_specs=in_specs, out_specs=(tokens,) * 5, check_vma=False)
```

```python
import functools
import math

import jax
import jax.numpy as jnp
from jax import lax
from jax.experimental import pallas as pl
from jax.experimental.pallas import tpu as pltpu
from jax.sharding import PartitionSpec as P

HD = 128
GROUP = 512
BPC = 64
CHIPS = 8
SCALE = 1.0 / math.sqrt(HD)
LOG2E = math.log2(math.e)
HIDDEN = 1e30
BF = jnp.bfloat16
F32 = jnp.float32


def nt(a, b):
    return lax.dot_general(a, b, (((1,), (1,)), ((), ())), preferred_element_type=F32)


def nn(a, b):
    return lax.dot_general(a, b, (((1,), (0,)), ((), ())), preferred_element_type=F32)


def tn(a, b):
    return lax.dot_general(a, b, (((0,), (0,)), ((), ())), preferred_element_type=F32)


def split(x, y):
    zero = jnp.zeros_like(x)
    return jnp.concatenate([jnp.concatenate([x, zero], axis=1), jnp.concatenate([zero, y], axis=1)], axis=0)


def stacked(x, y, b):
    rows = x.shape[0]
    both_heads = nn(jnp.concatenate([x, y], axis=0), b)
    return both_heads[:rows, :HD], both_heads[rows:, HD:]


def stats_kernel(
    place, q_any, g_any, o_any, ln_any, q_ref, g_ref, st_ref, o_ref, ln_ref, sems
):
    pairs = ((g_any, g_ref), (o_any, o_ref), (ln_any, ln_ref), (q_any, q_ref))
    copies = [pltpu.make_async_copy(src, dst, sems.at[i]) for i, (src, dst) in enumerate(pairs)]
    for copy in copies:
        copy.start()
    st_ref[2] = jnp.full(st_ref.shape[1:], place[2], jnp.int32).astype(F32)
    for copy in copies[:3]:
        copy.wait()
    st_ref[0] = ln_ref[...] * LOG2E
    for h in range(ln_ref.shape[0]):
        c = slice(h * HD, (h + 1) * HD)
        prod = g_ref[:, c].astype(F32) * o_ref[:, c].astype(F32)
        st_ref[1, h : h + 1, :] = jnp.sum(prod.T, axis=0, keepdims=True)
    for copy in copies[3:]:
        copy.wait()


def raw_kernel(q_ref, k_ref, v_ref, g_ref, st_ref, wait, dq_ref, dk_ref, dv_ref):
    block = 256
    tri = lax.broadcasted_iota(jnp.int32, (block, block), 0) <= lax.broadcasted_iota(
        jnp.int32, (block, block), 1
    )
    for h in range(0, st_ref.shape[1], 2):
        wide = slice(h * HD, (h + 2) * HD)
        q, k, v, g = q_ref[:, wide], k_ref[:, wide], v_ref[:, wide], g_ref[:, wide]
        ks, vs = ([x[:, :HD], x[:, HD:]] for x in (k, v))
        stripes = [[], []]
        for lo in range(0, GROUP, block):
            hi = lo + block
            s = nt(split(ks[0][lo:hi], ks[1][lo:hi]), q[lo:])
            d = nt(split(vs[0][lo:hi], vs[1][lo:hi]), g[lo:])
            weights, dscores = [], []
            for i in range(2):
                ln, delta = st_ref[0, h + i : h + i + 1, lo:], st_ref[1, h + i : h + i + 1, lo:]
                p = jnp.exp2(s[i * block : (i + 1) * block] * (SCALE * LOG2E) - ln)
                head = jnp.where(tri, p[:, :block], 0.0)
                p = head if hi == GROUP else jnp.concatenate([head, p[:, block:]], axis=1)
                dscores.append((p * (d[i * block : (i + 1) * block] - delta)).astype(BF))
                weights.append(p.astype(BF))
                stripes[i].append(dscores[i])
            dv, dk = stacked(*weights, g[lo:]), stacked(*dscores, q[lo:])
            dv_ref[lo:hi, wide] = jnp.concatenate(dv, axis=1).astype(BF)
            dk_ref[lo:hi, wide] = (jnp.concatenate(dk, axis=1) * SCALE).astype(BF)
        for i in range(2):
            c = slice((h + i) * HD, (h + i + 1) * HD)
            for lo in range(0, GROUP, block):
                hi = lo + block
                parts = [x[:, lo - j * block : hi - j * block] for j, x in enumerate(stripes[i][: hi // block])]
                ds = parts[0] if len(parts) == 1 else jnp.concatenate(parts, axis=0)
                dq_ref[lo:hi, c] = (tn(ks[i][:hi], ds) * SCALE).T


SMEM = pl.BlockSpec(memory_space=pltpu.SMEM)
VMEM = pl.BlockSpec(memory_space=pltpu.VMEM)
ANY = pl.BlockSpec(memory_space=pl.ANY)


def stats_call(place, arrays):
    heads = arrays[-1].shape[0]
    wide = (GROUP, heads * HD)
    return pl.pallas_call(
        stats_kernel,
        in_specs=[SMEM] + [ANY] * 4,
        out_specs=[VMEM] * 3,
        out_shape=[jax.ShapeDtypeStruct(wide, BF)] * 2
        + [jax.ShapeDtypeStruct((3, heads, GROUP), F32)],
        scratch_shapes=[
            pltpu.VMEM(wide, BF),
            pltpu.VMEM((heads, GROUP), F32),
            pltpu.SemaphoreType.DMA((4,)),
        ],
        compiler_params=pltpu.CompilerParams(vmem_limit_bytes=16 << 20),
        cost_estimate=pl.CostEstimate(
            flops=2 * heads * GROUP * HD, bytes_accessed=8 << 20, transcendentals=0
        ),
        name="stats",
    )(place, *[pltpu.with_memory_space_constraint(x, pltpu.HBM) for x in arrays])


def load_kernel(k_any, v_any, wait, k_ref, v_ref, sems):
    copies = [
        pltpu.make_async_copy(src, dst, sems.at[i]) for i, (src, dst) in enumerate(((k_any, k_ref), (v_any, v_ref)))
    ]
    for copy in copies:
        copy.start()
    for copy in copies:
        copy.wait()


def load_call(keys, values, wait):
    return pl.pallas_call(
        load_kernel,
        in_specs=[ANY] * 3,
        out_specs=[VMEM] * 2,
        out_shape=[jax.ShapeDtypeStruct(keys.shape, BF)] * 2,
        scratch_shapes=[pltpu.SemaphoreType.DMA((2,))],
        compiler_params=pltpu.CompilerParams(vmem_limit_bytes=8 << 20),
        cost_estimate=pl.CostEstimate(flops=0, bytes_accessed=4 << 20, transcendentals=0),
        name="load",
    )(*[pltpu.with_memory_space_constraint(x, pltpu.HBM) for x in (keys, values)], wait)


def raw_call(queries, keys, values, out_grad, stats, wait):
    heads = stats.shape[1]
    wide = queries.shape
    return pl.pallas_call(
        raw_kernel,
        in_specs=[VMEM] * 5 + [ANY],
        out_specs=[VMEM] * 3,
        out_shape=[jax.ShapeDtypeStruct(wide, kind) for kind in (F32, BF, BF)],
        compiler_params=pltpu.CompilerParams(vmem_limit_bytes=16 << 20),
        cost_estimate=pl.CostEstimate(
            flops=10 * heads * GROUP * GROUP * HD, bytes_accessed=10 << 20, transcendentals=heads * GROUP * GROUP
        ),
        name="raw_tokens",
    )(queries, keys, values, out_grad, stats, wait)


def beacon_kernel(shifts, waits, place, qh_ref, qp_ref, gh_ref, gp_ref, sh_ref, sp_ref, *refs):
    count = len(shifts)
    pieces, refs = refs[:count], refs[count + waits :]
    outs, ds_ref = refs[:count], refs[count]
    z, core = place[0], place[1]
    chunks = [z + shift for shift in shifts]
    sides = ((qh_ref, gh_ref, sh_ref, 2 * z + core), (qp_ref, gp_ref, sp_ref, 2 * z + 1 - core))

    def work():
        far = [
            [
                jnp.where((chunk >= 0) & (2 * chunk + core <= group), group - 2 * chunk - core, 2 * CHIPS)
                for chunk in chunks
            ]
            for *_, group in sides
        ]
        for h in range(0, sh_ref.shape[1], 2):
            wide = slice(h * HD, (h + 2) * HD)
            cs = [slice((h + i) * HD, (h + i + 1) * HD) for i in range(2)]
            rows = count * BPC
            kk = [jnp.concatenate([ref[0, :, c] for ref in pieces], axis=0) for c in cs]
            vv = [jnp.concatenate([ref[1, :, c] for ref in pieces], axis=0) for c in cs]
            if count > 1:
                kk, vv = split(*kk), split(*vv)
            total = None
            for side, (q_ref, g_ref, st_ref, _) in enumerate(sides):
                q, g = q_ref[:, wide], g_ref[:, wide]
                if count > 1:
                    s, d = nt(kk, q), nt(vv, g)
                    s, d = (s[:rows], s[rows:]), (d[:rows], d[rows:])
                else:
                    s = nt(kk[0], q[:, :HD]), nt(kk[1], q[:, HD:])
                    d = nt(vv[0], g[:, :HD]), nt(vv[1], g[:, HD:])
                weights, dscores = [], []
                for i in range(2):
                    ln, delta, reach = (st_ref[n, h + i : h + i + 1, :] for n in range(3))
                    bias = jnp.concatenate(
                        [
                            jnp.broadcast_to(
                                jnp.where(reach > jnp.full((1, GROUP), f, jnp.int32).astype(F32), ln, HIDDEN),
                                (BPC, GROUP),
                            )
                            for f in far[side]
                        ],
                        axis=0,
                    )
                    p = jnp.exp2(s[i] * (SCALE * LOG2E) - bias)
                    dscores.append((p * (d[i] - delta)).astype(BF))
                    weights.append(p.astype(BF))
                    ds_ref[h + i, :, side * GROUP : (side + 1) * GROUP] = dscores[i]
                parts = stacked(*dscores, q) + stacked(*weights, g)
                total = parts if total is None else [x + y for x, y in zip(total, parts, strict=True)]
            for i, c in enumerate(cs):
                dk, dv = total[i] * SCALE, total[2 + i]
                for n, ref in enumerate(outs):
                    ref[0, :, c] = dk[n * BPC : (n + 1) * BPC].astype(ref.dtype)
                    ref[1, :, c] = dv[n * BPC : (n + 1) * BPC].astype(ref.dtype)

    if 0 in shifts:
        work()
        return
    valid = functools.reduce(jnp.logical_or, [chunk >= 0 for chunk in chunks])
    pl.when(valid)(work)

    @pl.when(jnp.logical_not(valid))
    def _():
        for ref in outs:
            ref[...] = jnp.zeros_like(ref)
        ds_ref[...] = jnp.zeros_like(ds_ref)


def beacon_call(place, sides, parts, waits, name):
    pieces, shifts, kinds = zip(*parts, strict=True)
    heads = sides[4].shape[1]
    count = len(pieces)
    items = heads * 2 * GROUP * count * BPC
    return pl.pallas_call(
        functools.partial(beacon_kernel, shifts, len(waits)),
        in_specs=[SMEM] + [VMEM] * (6 + count) + [ANY] * len(waits),
        out_specs=[VMEM] * (count + 1),
        out_shape=[jax.ShapeDtypeStruct((2, BPC, heads * HD), kind) for kind in kinds]
        + [jax.ShapeDtypeStruct((heads, count * BPC, 2 * GROUP), BF)],
        compiler_params=pltpu.CompilerParams(vmem_limit_bytes=16 << 20),
        cost_estimate=pl.CostEstimate(flops=8 * items * HD, bytes_accessed=8 << 20, transcendentals=items),
        name=name,
    )(place, *sides, *pieces, *waits)


def query_kernel(steps, *refs):
    ds_refs, k_refs, outs = refs[:steps], refs[steps:-2], refs[-2:]
    for h in range(ds_refs[0].shape[0]):
        c = slice(h * HD, (h + 1) * HD)
        kk = jnp.concatenate([ref[0, :, c] for ref in k_refs], axis=0)
        for side, out in enumerate(outs):
            ds = jnp.concatenate([ref[h, :, side * GROUP : (side + 1) * GROUP] for ref in ds_refs], axis=0)
            out[:, c] = (tn(kk, ds) * SCALE).T.astype(out.dtype)


def query_call(ds_list, pieces):
    heads = ds_list[0].shape[0]
    rows = sum(ds.shape[1] for ds in ds_list)
    return pl.pallas_call(
        functools.partial(query_kernel, len(ds_list)),
        in_specs=[VMEM] * (len(ds_list) + len(pieces)),
        out_specs=[VMEM] * 2,
        out_shape=[jax.ShapeDtypeStruct((GROUP, heads * HD), kind) for kind in (F32, BF)],
        compiler_params=pltpu.CompilerParams(vmem_limit_bytes=16 << 20),
        cost_estimate=pl.CostEstimate(
            flops=2 * heads * rows * 2 * GROUP * HD, bytes_accessed=16 << 20, transcendentals=0
        ),
        name="query_grad",
    )(*ds_list, *pieces)


def join(array, *after):
    return pl.pallas_call(
        lambda *refs: None,
        in_specs=[ANY] * (1 + len(after)),
        out_specs=ANY,
        out_shape=jax.ShapeDtypeStruct(array.shape, array.dtype),
        input_output_aliases={0: 0},
        compiler_params=pltpu.CompilerParams(vmem_limit_bytes=1 << 20),
        name="join",
    )(array, *after)


def both(a, b, *after):
    a = join(a, b, *after)
    return a, join(b, a)


def at(z, core):
    return 2 * (z % CHIPS) + core


SWAP = [(at(z, core), at(z, 1 - core)) for z in range(CHIPS) for core in (0, 1)]


UP = [(at(z, core), at(z + 1, core)) for z in range(CHIPS) for core in (0, 1)]
DOWN = [(at(z, core), at(z - 1, core)) for z in range(CHIPS) for core in (0, 1)]


def local(
    queries, keys, values, out_grad, forward_out, log_norm, beacon_keys, beacon_values, beacon_reach
):
    ctx = lax.axis_index("ctx").astype(jnp.int32)
    place = jnp.stack([ctx // 2, ctx % 2, beacon_reach[0].astype(jnp.int32)])
    send = functools.partial(lax.ppermute, axis_name="ctx")
    own = jnp.stack([beacon_keys, beacon_values])
    a1, b1 = send(own, perm=UP), send(own, perm=DOWN)
    queries_other, grad_other = send(queries, perm=SWAP), send(out_grad, perm=SWAP)
    q_home, g_home, stats = stats_call(place, (queries, out_grad, forward_out, log_norm))
    sides = (q_home, queries_other, g_home, grad_other, stats, send(stats, perm=SWAP))
    a1, b1 = both(a1, b1, sides[5])
    a2, b2 = send(a1, perm=UP), send(b1, perm=DOWN)
    t1a, t1b, t0, ds1 = beacon_call(
        place, sides, ((a1, -1, F32), (b1, 1 - CHIPS, F32), (own, 0, F32)), (), "beacons_near"
    )
    a2, b2 = both(a2, b2, ds1)
    a3, b3 = send(a2, perm=UP), send(b2, perm=DOWN)
    t2a, t2b, ds2 = beacon_call(place, sides, ((a2, -2, F32), (b2, 2 - CHIPS, F32)), (), "beacons_second")
    a3, b3 = both(a3, b3, ds2)
    a4 = send(a3, perm=UP)
    t3a, t3b, ds3 = beacon_call(place, sides, ((a3, -3, F32), (b3, 3 - CHIPS, BF)), (), "beacons_third")
    t4, ds4 = beacon_call(place, sides, ((a4, -4, BF),), (ds3,), "beacons_far")

    def plus(arrived, term):
        return (arrived.astype(F32) + term).astype(BF)

    a = send(t4, perm=DOWN)
    dq_home, dq_other = query_call((ds1, ds2, ds3, ds4), (a1, b1, own, a2, b2, a3, b3, a4))
    k_home, v_home = load_call(keys, values, t4)
    a, b = both(a, t3b, dq_other, k_home)
    a, b = send(plus(a, t3a), perm=DOWN), send(b, perm=UP)
    dq_raw, key_grad, value_grad = raw_call(q_home, k_home, v_home, g_home, stats, dq_other)
    a, b = both(a, b, dq_raw)
    a, b = send(plus(a, t2a), perm=DOWN), send(plus(b, t2b), perm=UP)
    query_grad = (dq_raw + dq_home + send(dq_other, perm=SWAP).astype(F32)).astype(BF)
    a, b = both(a, b, query_grad)
    a, b = send(plus(a, t1a), perm=DOWN), send(plus(b, t1b), perm=UP)
    total = (t0 + (a.astype(F32) + b.astype(F32))).astype(BF)
    return query_grad, key_grad, value_grad, total[0], total[1]


def solution(mesh):
    tokens = P(("dp", "ctx"), "head")
    in_specs = (tokens,) * 5 + (P("head", ("dp", "ctx")), tokens, tokens, P(("dp", "ctx")))
    return jax.shard_map(local, mesh=mesh, in_specs=in_specs, out_specs=(tokens,) * 5, check_vma=False)
```

```python
import functools
import math

import jax
import jax.numpy as jnp
from jax import lax
from jax.experimental import pallas as pl
from jax.experimental.pallas import tpu as pltpu
from jax.sharding import PartitionSpec as P

HD = 128
GROUP = 512
BPC = 64
CHIPS = 8
SCALE = 1.0 / math.sqrt(HD)
LOG2E = math.log2(math.e)
HIDDEN = 1e30
BF = jnp.bfloat16
F32 = jnp.float32


def nt(a, b):
    return lax.dot_general(a, b, (((1,), (1,)), ((), ())), preferred_element_type=F32)


def nn(a, b):
    return lax.dot_general(a, b, (((1,), (0,)), ((), ())), preferred_element_type=F32)


def tn(a, b):
    return lax.dot_general(a, b, (((0,), (0,)), ((), ())), preferred_element_type=F32)


def split(x, y):
    zero = jnp.zeros_like(x)
    return jnp.concatenate([jnp.concatenate([x, zero], axis=1), jnp.concatenate([zero, y], axis=1)], axis=0)


def stacked(x, y, b):
    rows = x.shape[0]
    both_heads = nn(jnp.concatenate([x, y], axis=0), b)
    return both_heads[:rows, :HD], both_heads[rows:, HD:]


def stats_kernel(
    place, q_any, g_any, o_any, ln_any, q_ref, g_ref, st_ref, o_ref, ln_ref, sems
):
    pairs = ((g_any, g_ref), (o_any, o_ref), (ln_any, ln_ref), (q_any, q_ref))
    copies = [pltpu.make_async_copy(src, dst, sems.at[i]) for i, (src, dst) in enumerate(pairs)]
    for copy in copies:
        copy.start()
    st_ref[2] = jnp.full(st_ref.shape[1:], place[2], jnp.int32).astype(F32)
    for copy in copies[:3]:
        copy.wait()
    st_ref[0] = ln_ref[...] * LOG2E
    for h in range(ln_ref.shape[0]):
        c = slice(h * HD, (h + 1) * HD)
        prod = g_ref[:, c].astype(F32) * o_ref[:, c].astype(F32)
        st_ref[1, h : h + 1, :] = jnp.sum(prod.T, axis=0, keepdims=True)
    for copy in copies[3:]:
        copy.wait()


def raw_kernel(q_ref, k_ref, v_ref, g_ref, st_ref, wait, dq_ref, dk_ref, dv_ref):
    block = 256
    tri = lax.broadcasted_iota(jnp.int32, (block, block), 0) <= lax.broadcasted_iota(
        jnp.int32, (block, block), 1
    )
    for h in range(0, st_ref.shape[1], 2):
        wide = slice(h * HD, (h + 2) * HD)
        q, k, v, g = q_ref[:, wide], k_ref[:, wide], v_ref[:, wide], g_ref[:, wide]
        ks, vs = ([x[:, :HD], x[:, HD:]] for x in (k, v))
        stripes = [[], []]
        for lo in range(0, GROUP, block):
            hi = lo + block
            s = nt(split(ks[0][lo:hi], ks[1][lo:hi]), q[lo:])
            d = nt(split(vs[0][lo:hi], vs[1][lo:hi]), g[lo:])
            weights, dscores = [], []
            for i in range(2):
                ln, delta = st_ref[0, h + i : h + i + 1, lo:], st_ref[1, h + i : h + i + 1, lo:]
                p = jnp.exp2(s[i * block : (i + 1) * block] * (SCALE * LOG2E) - ln)
                head = jnp.where(tri, p[:, :block], 0.0)
                p = head if hi == GROUP else jnp.concatenate([head, p[:, block:]], axis=1)
                dscores.append((p * (d[i * block : (i + 1) * block] - delta)).astype(BF))
                weights.append(p.astype(BF))
                stripes[i].append(dscores[i])
            dv, dk = stacked(*weights, g[lo:]), stacked(*dscores, q[lo:])
            dv_ref[lo:hi, wide] = jnp.concatenate(dv, axis=1).astype(BF)
            dk_ref[lo:hi, wide] = (jnp.concatenate(dk, axis=1) * SCALE).astype(BF)
        for i in range(2):
            c = slice((h + i) * HD, (h + i + 1) * HD)
            for lo in range(0, GROUP, block):
                hi = lo + block
                parts = [x[:, lo - j * block : hi - j * block] for j, x in enumerate(stripes[i][: hi // block])]
                ds = parts[0] if len(parts) == 1 else jnp.concatenate(parts, axis=0)
                dq_ref[lo:hi, c] = (tn(ks[i][:hi], ds) * SCALE).T


SMEM = pl.BlockSpec(memory_space=pltpu.SMEM)
VMEM = pl.BlockSpec(memory_space=pltpu.VMEM)
ANY = pl.BlockSpec(memory_space=pl.ANY)


def stats_call(place, arrays):
    heads = arrays[-1].shape[0]
    wide = (GROUP, heads * HD)
    return pl.pallas_call(
        stats_kernel,
        in_specs=[SMEM] + [ANY] * 4,
        out_specs=[VMEM] * 3,
        out_shape=[jax.ShapeDtypeStruct(wide, BF)] * 2
        + [jax.ShapeDtypeStruct((3, heads, GROUP), F32)],
        scratch_shapes=[
            pltpu.VMEM(wide, BF),
            pltpu.VMEM((heads, GROUP), F32),
            pltpu.SemaphoreType.DMA((4,)),
        ],
        compiler_params=pltpu.CompilerParams(vmem_limit_bytes=16 << 20),
        cost_estimate=pl.CostEstimate(
            flops=2 * heads * GROUP * HD, bytes_accessed=8 << 20, transcendentals=0
        ),
        name="stats",
    )(place, *[pltpu.with_memory_space_constraint(x, pltpu.HBM) for x in arrays])


def load_kernel(k_any, v_any, wait, k_ref, v_ref, sems):
    copies = [
        pltpu.make_async_copy(src, dst, sems.at[i]) for i, (src, dst) in enumerate(((k_any, k_ref), (v_any, v_ref)))
    ]
    for copy in copies:
        copy.start()
    for copy in copies:
        copy.wait()


def load_call(keys, values, wait):
    return pl.pallas_call(
        load_kernel,
        in_specs=[ANY] * 3,
        out_specs=[VMEM] * 2,
        out_shape=[jax.ShapeDtypeStruct(keys.shape, BF)] * 2,
        scratch_shapes=[pltpu.SemaphoreType.DMA((2,))],
        compiler_params=pltpu.CompilerParams(vmem_limit_bytes=8 << 20),
        cost_estimate=pl.CostEstimate(flops=0, bytes_accessed=4 << 20, transcendentals=0),
        name="load",
    )(*[pltpu.with_memory_space_constraint(x, pltpu.HBM) for x in (keys, values)], wait)


def raw_call(queries, keys, values, out_grad, stats, wait):
    heads = stats.shape[1]
    wide = queries.shape
    return pl.pallas_call(
        raw_kernel,
        in_specs=[VMEM] * 5 + [ANY],
        out_specs=[VMEM] * 3,
        out_shape=[jax.ShapeDtypeStruct(wide, kind) for kind in (F32, BF, BF)],
        compiler_params=pltpu.CompilerParams(vmem_limit_bytes=16 << 20),
        cost_estimate=pl.CostEstimate(
            flops=10 * heads * GROUP * GROUP * HD, bytes_accessed=10 << 20, transcendentals=heads * GROUP * GROUP
        ),
        name="raw_tokens",
    )(queries, keys, values, out_grad, stats, wait)


def beacon_kernel(shifts, waits, place, qh_ref, qp_ref, gh_ref, gp_ref, sh_ref, sp_ref, *refs):
    count = len(shifts)
    pieces, refs = refs[:count], refs[count + waits :]
    outs, ds_ref = refs[:count], refs[count]
    z, core = place[0], place[1]
    chunks = [z + shift for shift in shifts]
    sides = ((qh_ref, gh_ref, sh_ref, 2 * z + core), (qp_ref, gp_ref, sp_ref, 2 * z + 1 - core))

    def work():
        far = [
            [
                jnp.where((chunk >= 0) & (2 * chunk + core <= group), group - 2 * chunk - core, 2 * CHIPS)
                for chunk in chunks
            ]
            for *_, group in sides
        ]
        for h in range(0, sh_ref.shape[1], 2):
            wide = slice(h * HD, (h + 2) * HD)
            cs = [slice((h + i) * HD, (h + i + 1) * HD) for i in range(2)]
            rows = count * BPC
            kk = [jnp.concatenate([ref[0, :, c] for ref in pieces], axis=0) for c in cs]
            vv = [jnp.concatenate([ref[1, :, c] for ref in pieces], axis=0) for c in cs]
            if count > 1:
                kk, vv = split(*kk), split(*vv)
            total = None
            for side, (q_ref, g_ref, st_ref, _) in enumerate(sides):
                q, g = q_ref[:, wide], g_ref[:, wide]
                if count > 1:
                    s, d = nt(kk, q), nt(vv, g)
                    s, d = (s[:rows], s[rows:]), (d[:rows], d[rows:])
                else:
                    s = nt(kk[0], q[:, :HD]), nt(kk[1], q[:, HD:])
                    d = nt(vv[0], g[:, :HD]), nt(vv[1], g[:, HD:])
                weights, dscores = [], []
                for i in range(2):
                    ln, delta, reach = (st_ref[n, h + i : h + i + 1, :] for n in range(3))
                    bias = jnp.concatenate(
                        [
                            jnp.broadcast_to(
                                jnp.where(reach > jnp.full((1, GROUP), f, jnp.int32).astype(F32), ln, HIDDEN),
                                (BPC, GROUP),
                            )
                            for f in far[side]
                        ],
                        axis=0,
                    )
                    p = jnp.exp2(s[i] * (SCALE * LOG2E) - bias)
                    dscores.append((p * (d[i] - delta)).astype(BF))
                    weights.append(p.astype(BF))
                    ds_ref[h + i, :, side * GROUP : (side + 1) * GROUP] = dscores[i]
                parts = stacked(*dscores, q) + stacked(*weights, g)
                total = parts if total is None else [x + y for x, y in zip(total, parts, strict=True)]
            for i, c in enumerate(cs):
                dk, dv = total[i] * SCALE, total[2 + i]
                for n, ref in enumerate(outs):
                    ref[0, :, c] = dk[n * BPC : (n + 1) * BPC].astype(ref.dtype)
                    ref[1, :, c] = dv[n * BPC : (n + 1) * BPC].astype(ref.dtype)

    if 0 in shifts:
        work()
        return
    valid = functools.reduce(jnp.logical_or, [chunk >= 0 for chunk in chunks])
    pl.when(valid)(work)

    @pl.when(jnp.logical_not(valid))
    def _():
        for ref in outs:
            ref[...] = jnp.zeros_like(ref)
        ds_ref[...] = jnp.zeros_like(ds_ref)


def beacon_call(place, sides, parts, waits, name):
    pieces, shifts, kinds = zip(*parts, strict=True)
    heads = sides[4].shape[1]
    count = len(pieces)
    items = heads * 2 * GROUP * count * BPC
    return pl.pallas_call(
        functools.partial(beacon_kernel, shifts, len(waits)),
        in_specs=[SMEM] + [VMEM] * (6 + count) + [ANY] * len(waits),
        out_specs=[VMEM] * (count + 1),
        out_shape=[jax.ShapeDtypeStruct((2, BPC, heads * HD), kind) for kind in kinds]
        + [jax.ShapeDtypeStruct((heads, count * BPC, 2 * GROUP), BF)],
        compiler_params=pltpu.CompilerParams(vmem_limit_bytes=16 << 20),
        cost_estimate=pl.CostEstimate(flops=8 * items * HD, bytes_accessed=8 << 20, transcendentals=items),
        name=name,
    )(place, *sides, *pieces, *waits)


def query_kernel(steps, *refs):
    ds_refs, k_refs, outs = refs[:steps], refs[steps:-2], refs[-2:]
    for h in range(ds_refs[0].shape[0]):
        c = slice(h * HD, (h + 1) * HD)
        kk = jnp.concatenate([ref[0, :, c] for ref in k_refs], axis=0)
        for side, out in enumerate(outs):
            ds = jnp.concatenate([ref[h, :, side * GROUP : (side + 1) * GROUP] for ref in ds_refs], axis=0)
            out[:, c] = (tn(kk, ds) * SCALE).T.astype(out.dtype)


def query_call(ds_list, pieces):
    heads = ds_list[0].shape[0]
    rows = sum(ds.shape[1] for ds in ds_list)
    return pl.pallas_call(
        functools.partial(query_kernel, len(ds_list)),
        in_specs=[VMEM] * (len(ds_list) + len(pieces)),
        out_specs=[VMEM] * 2,
        out_shape=[jax.ShapeDtypeStruct((GROUP, heads * HD), kind) for kind in (F32, BF)],
        compiler_params=pltpu.CompilerParams(vmem_limit_bytes=16 << 20),
        cost_estimate=pl.CostEstimate(
            flops=2 * heads * rows * 2 * GROUP * HD, bytes_accessed=16 << 20, transcendentals=0
        ),
        name="query_grad",
    )(*ds_list, *pieces)


def join(array, *after):
    return pl.pallas_call(
        lambda *refs: None,
        in_specs=[ANY] * (1 + len(after)),
        out_specs=ANY,
        out_shape=jax.ShapeDtypeStruct(array.shape, array.dtype),
        input_output_aliases={0: 0},
        compiler_params=pltpu.CompilerParams(vmem_limit_bytes=1 << 20),
        name="join",
    )(array, *after)


def both(a, b, *after):
    a = join(a, b, *after)
    return a, join(b, a)


def at(z, core):
    return 2 * (z % CHIPS) + core


SWAP = [(at(z, core), at(z, 1 - core)) for z in range(CHIPS) for core in (0, 1)]


UP = [(at(z, core), at(z + 1, core)) for z in range(CHIPS) for core in (0, 1)]
DOWN = [(at(z, core), at(z - 1, core)) for z in range(CHIPS) for core in (0, 1)]


def local(
    queries, keys, values, out_grad, forward_out, log_norm, beacon_keys, beacon_values, beacon_reach
):
    ctx = lax.axis_index("ctx").astype(jnp.int32)
    place = jnp.stack([ctx // 2, ctx % 2, beacon_reach[0].astype(jnp.int32)])
    send = functools.partial(lax.ppermute, axis_name="ctx")
    own = jnp.stack([beacon_keys, beacon_values])
    a1, b1 = send(own, perm=UP), send(own, perm=DOWN)
    queries_other, grad_other = send(queries, perm=SWAP), send(out_grad, perm=SWAP)
    q_home, g_home, stats = stats_call(place, (queries, out_grad, forward_out, log_norm))
    sides = (q_home, queries_other, g_home, grad_other, stats, send(stats, perm=SWAP))
    a1, b1 = both(a1, b1, sides[5])
    a2, b2 = send(a1, perm=UP), send(b1, perm=DOWN)
    t1a, t1b, t0, ds1 = beacon_call(
        place, sides, ((a1, -1, F32), (b1, 1 - CHIPS, F32), (own, 0, F32)), (), "beacons_near"
    )
    a2, b2 = both(a2, b2, ds1)
    a3, b3 = send(a2, perm=UP), send(b2, perm=DOWN)
    t2a, t2b, ds2 = beacon_call(place, sides, ((a2, -2, F32), (b2, 2 - CHIPS, F32)), (), "beacons_second")
    a3, b3 = both(a3, b3, ds2)
    a4 = send(a3, perm=UP)
    t3a, t3b, ds3 = beacon_call(place, sides, ((a3, -3, F32), (b3, 3 - CHIPS, BF)), (), "beacons_third")
    t4, ds4 = beacon_call(place, sides, ((a4, -4, BF),), (ds3,), "beacons_far")

    def plus(arrived, term):
        return (arrived.astype(F32) + term).astype(BF)

    a = send(t4, perm=DOWN)
    dq_home, dq_other = query_call((ds1, ds2, ds3, ds4), (a1, b1, own, a2, b2, a3, b3, a4))
    k_home, v_home = load_call(keys, values, t4)
    a, b = both(a, t3b, dq_other, k_home)
    a, b = send(plus(a, t3a), perm=DOWN), send(b, perm=UP)
    dq_raw, key_grad, value_grad = raw_call(q_home, k_home, v_home, g_home, stats, dq_other)
    a, b = both(a, b, dq_raw)
    b, a = send(plus(b, t2b), perm=UP), send(plus(a, t2a), perm=DOWN)
    query_grad = (dq_raw + dq_home + send(dq_other, perm=SWAP).astype(F32)).astype(BF)
    a, b = both(a, b, query_grad)
    b, a = send(plus(b, t1b), perm=UP), send(plus(a, t1a), perm=DOWN)
    total = (t0 + (a.astype(F32) + b.astype(F32))).astype(BF)
    return query_grad, key_grad, value_grad, total[0], total[1]


def solution(mesh):
    tokens = P(("dp", "ctx"), "head")
    in_specs = (tokens,) * 5 + (P("head", ("dp", "ctx")), tokens, tokens, P(("dp", "ctx")))
    return jax.shard_map(local, mesh=mesh, in_specs=in_specs, out_specs=(tokens,) * 5, check_vma=False)
```
